32 devices in a mesh: gx: 4 (over y, x), gy: 8 (over z, core).
Axes of the slice: x: 2, y: 2, z: 4, core: 2. Of those that a mesh axis runs over, the one named last changes fastest.
Arguments:
- coords: float32 [3, 131072], P(None, ('gx', 'gy')), may hold values from 0 to 8
- noise: float32 [131072], P(('gx', 'gy')), may hold values from 0.5 to 2
- order: int32 [4, 32768], P('gx', 'gy'), may hold values from 0 to 32767, as said below
- probes: bfloat16 [64, 131072], P(None, ('gx', 'gy')), may hold values from -5 to 5
- factors: bfloat16 [7, 2, 32, 131072], P(None, None, None, ('gx', 'gy')), may hold values from -1 to 1
Outputs:
- product: float32 [64, 131072], P(None, ('gx', 'gy'))
The draws below stay inside these ranges and needn't reach their ends.
Inputs may be any that keep to these rules, and one draw needn't show every extreme that they name: Each row of order lists every number from 0 to 32767 once; every run of 4096 tree positions starting at a multiple of 4096 takes exactly 512 numbers from each run of 4096 input indices starting at a multiple of 4096.
All inputs are finite; a program needn't handle non-finite values.
Results may differ from the reference program's by a relative error of at most 0.0029.
Values may be sent and summed in bfloat16 or wider, within the bound.
No kernel may reach another device: no remote copies, remote signals or barrier semaphores. Data moves between devices by JAX's collectives and lax.ppermute only.
A program may use at most 128 MiB of HBM per device.

```python
import math
import jax
import jax.numpy as jnp
from jax import lax

LEAF = 1024
RANK = 32
PROBES = 64
PTS_DEV = 4096
NPTS = 131072
GROUP = 32768
LEVELS = 7


def draw_factors(key, part):
    key = jax.random.fold_in(key, 7)
    layers = []
    for tier_index in range(LEVELS):
        tier_key = jax.random.fold_in(key, tier_index)
        scale = (0.5 / (RANK * LEAF * 2.0 ** tier_index) ** 0.5) ** 0.5
        base = jax.random.normal(tier_key, (2, RANK, NPTS), jnp.float32)
        layers.append((base * scale).astype(jnp.bfloat16))
    return jnp.stack(layers)


def draw_order(key, part):
    key = jax.random.fold_in(key, 11)
    groups = NPTS // GROUP
    inner = GROUP // PTS_DEV
    slot_size = PTS_DEV // inner
    owner_keys = jax.random.split(jax.random.fold_in(key, 1), groups * inner)
    owner_perms = jax.vmap(lambda one_key: jax.random.permutation(one_key, PTS_DEV))(owner_keys)
    owner_perms = owner_perms.astype(jnp.int32).reshape(groups, inner, inner, slot_size)
    owner_base = (jnp.arange(inner, dtype=jnp.int32) * PTS_DEV)[None, :, None, None]
    picked = (owner_perms + owner_base).transpose(0, 2, 1, 3).reshape(groups * inner, PTS_DEV)
    place_keys = jax.random.split(jax.random.fold_in(key, 2), groups * inner)
    places = jax.vmap(lambda one_key: jax.random.permutation(one_key, PTS_DEV))(place_keys).astype(jnp.int32)
    shuffled = jnp.take_along_axis(picked, places, axis=1)
    return shuffled.reshape(groups, GROUP)


def block_levels(own_key, extent, pieces, least, largest):
    loudness = 1.0
    for axis_at, blocks in pieces:
        heights = jax.random.uniform(jax.random.fold_in(jax.random.fold_in(own_key, 6), axis_at), (blocks,), jnp.float32, least / len(pieces), largest / len(pieces))
        loudness = loudness * jnp.repeat(jnp.exp(heights), extent[axis_at] // blocks).reshape((-1,) + (1,) * (len(extent) - 1 - axis_at))
    return loudness


def bell_draw(rng, shape, deviation, reach, pieces=(), held_as=jnp.bfloat16):
    values = jax.random.normal(rng, shape, jnp.float32) * deviation
    if len(pieces) > 0:
        values = block_levels(rng, shape, pieces, -0.22, 0.18) * values
    return jnp.clip(values, min=-reach, max=reach).astype(held_as)


def setup_inputs(seed: int = 0) -> dict:
    key_of = jax.random.split(jax.random.key(seed), 6)
    coords = jnp.clip(8.0 * jax.random.uniform(key_of[0], (3, NPTS), jnp.float32) ** block_levels(key_of[0], (3, NPTS), ((1, 32),), -0.2, 0.2), 0.0, 8.0)
    noise = jnp.clip(jnp.exp(math.log(2.0) - 1.3862944 * jax.random.uniform(key_of[1], (NPTS,), jnp.float32) ** block_levels(key_of[1], (NPTS,), ((0, 32),), -0.2, 0.2)), 0.5, 2.0)
    order = draw_order(jax.random.fold_in(key_of[5], 71), 0)
    probes = bell_draw(key_of[3], (PROBES, NPTS), 1.0, 5.0, ((1, 32),))
    factors = draw_factors(jax.random.fold_in(key_of[5], 71), 0)
    return dict(coords=coords, noise=noise, order=order, probes=probes, factors=factors)


SQRT_THREE = 1.7320508075688772

def leaf_kernel(spots, spread):
    square = (spots[0][:, None] - spots[0][None, :]) ** 2
    square = square + (spots[1][:, None] - spots[1][None, :]) ** 2
    square = square + (spots[2][:, None] - spots[2][None, :]) ** 2
    scaled = jnp.sqrt(square) * SQRT_THREE
    return ((1.0 + scaled) * jnp.exp(-scaled) + jnp.diag(spread)).astype(jnp.bfloat16)

def level_term(pair, probes, width):
    total = probes.shape[1]
    nodes = total // width
    right = pair[1].astype(jnp.float32).reshape(RANK, nodes, width)
    left = pair[0].astype(jnp.float32).reshape(RANK, nodes, width)
    vectors = probes.astype(jnp.float32).reshape(PROBES, nodes, width)
    coeff = jnp.einsum('rkn,pkn->krp', right, vectors)
    sibling = coeff.reshape(nodes // 2, 2, RANK, PROBES)[:, ::-1].reshape(nodes, RANK, PROBES).astype(jnp.bfloat16)
    return jnp.einsum('rkn,krp->pkn', left, sibling.astype(jnp.float32)).reshape(PROBES, total)

def reference(coords, noise, order, probes, factors):
    groups = order.shape[0]
    group_size = order.shape[1]
    grouped = coords.reshape(3, groups, group_size)
    tree_coords = jnp.take_along_axis(grouped, order[None, :, :], axis=2).reshape(3, NPTS)
    tree_noise = jnp.take_along_axis(noise.reshape(groups, group_size), order, axis=1).reshape(NPTS)
    leaves = NPTS // LEAF
    leaf_coords = tree_coords.reshape(3, leaves, LEAF).transpose(1, 0, 2)
    leaf_noise = tree_noise.reshape(leaves, LEAF)
    leaf_probes = probes.reshape(PROBES, leaves, LEAF).transpose(1, 0, 2)

    def one_leaf(items):
        spots, spread, vectors = items
        return jnp.dot(vectors, leaf_kernel(spots, spread), preferred_element_type=jnp.float32)
    dense = lax.map(one_leaf, (leaf_coords, leaf_noise, leaf_probes))
    product = dense.transpose(1, 0, 2).reshape(PROBES, NPTS)
    for tier_index in range(LEVELS):
        product = product + level_term(factors[tier_index], probes, LEAF * 2 ** tier_index)
    return product
```

```python
import functools

import jax
import jax.numpy as jnp
from jax import lax
from jax.experimental import pallas as pl
from jax.experimental.pallas import tpu as pltpu
from jax.sharding import PartitionSpec as P

LEAF = 1024
TILE = 256
LANES = 256
STRIP = 128
NOISE_SCALE = 65535.0 / 2.0
OFFSET = 32768.0
SQRT_THREE = 1.7320508075688772
LOG2_E = 1.4426950408889634
LN_2 = 0.6931471805599453
LOG2_LN_2 = -0.5287663729448977
FEATURE_STEP = 2.0**-11
COORD_SCALE = SQRT_THREE * LOG2_E / FEATURE_STEP
COORD_MIDDLE = 80.0
COEFF_STEPS = 32760.0
MIB = 1024 * 1024


def exchanged(array, axis, mask):
    return lax.ppermute(array, axis, [(i, i ^ mask) for i in range(lax.axis_size(axis))])


def rounded_up(value, multiple):
    return -(-value // multiple) * multiple


def message_width(rank, outer_bits):
    return rounded_up(rank * (2 + outer_bits), 128)


def message_kernel(local_levels, inner_bits, factors_ref, probes_ref, coords_ref, noise_ref, *rest):
    message_refs, (right, vectors, spots, spread, right_sems, vector_sems, point_sems) = (
        rest[:-7],
        rest[-7:],
    )
    _, _, rank, points = factors_ref.shape
    count = probes_ref.shape[0]
    leaves = points // LEAF
    heights = right.shape[1]
    outer_bits = heights - inner_bits
    point_copies = [
        pltpu.make_async_copy(coords_ref, spots, point_sems.at[0]),
        pltpu.make_async_copy(noise_ref, spread, point_sems.at[1]),
    ]
    copies = []
    for leaf in range(leaves):
        span = pl.ds(leaf * LEAF, LEAF)
        copies.append(
            (
                pltpu.make_async_copy(
                    factors_ref.at[pl.ds(local_levels, heights), 1, :, span],
                    right.at[leaf],
                    right_sems.at[leaf],
                ),
                pltpu.make_async_copy(
                    probes_ref.at[:, span], vectors.at[leaf], vector_sems.at[leaf]
                ),
            )
        )
    for copy in point_copies:
        copy.start()
    for pair in copies:
        pair[0].start()
        pair[1].start()
    for copy in point_copies:
        copy.wait()

    sub = points // LANES
    lines = []
    for which in range(4):
        source = spots if which < 3 else spread
        scale = COORD_SCALE if which < 3 else NOISE_SCALE
        line = which if which < 3 else 0
        for at in range(sub):
            lines.append(source[line : line + 1, at * LANES : (at + 1) * LANES] * scale)
    coded = (jnp.round(jnp.concatenate(lines, axis=0)) - OFFSET).astype(jnp.int32).astype(jnp.int16)
    for message_ref in message_refs:
        message_ref[: 4 * sub] = coded

    upper = None
    for leaf in range(leaves):
        copies[leaf][0].wait()
        copies[leaf][1].wait()
        part = lax.dot_general(
            right[leaf].reshape(heights * rank, LEAF),
            vectors[leaf],
            (((1,), (1,)), ((), ())),
            preferred_element_type=jnp.float32,
        )
        upper = part if upper is None else upper + part
    upper = upper.T

    largest = jnp.max(jnp.abs(upper), axis=0, keepdims=True)
    power = jnp.ceil(jnp.log(jnp.maximum(largest, 2.0**-60)) * LOG2_E)
    fixed = jnp.round(upper * (COEFF_STEPS * jnp.exp2(-power)))
    wide = message_width(rank, outer_bits)
    pieces_across = LANES // wide
    tall = count // pieces_across
    for height, message_ref in enumerate(message_refs):
        chosen = [height] + list(range(inner_bits, heights))
        spans = [slice(height * rank, (height + 1) * rank) for height in chosen]
        powers = [power[:, span] for span in spans]
        powers.append(jnp.zeros((count - len(spans), rank), jnp.float32))
        body = [fixed[:, span] for span in spans] + [jnp.concatenate(powers, axis=0)]
        if wide > rank * len(body):
            body.append(jnp.zeros((count, wide - rank * len(body)), jnp.float32))
        body = jnp.concatenate(body, axis=1)
        body = jnp.concatenate(
            [body[at * tall : (at + 1) * tall] for at in range(pieces_across)], axis=1
        )
        message_ref[4 * sub :] = body.astype(jnp.int32).astype(jnp.int16)


def messages(coords, noise, factors, probes, local_levels, inner_bits):
    levels, _, rank, points = factors.shape
    count = probes.shape[0]
    leaves = points // LEAF
    heights = levels - local_levels
    wide = message_width(rank, heights - inner_bits)
    rows = (4 * points + count * wide) // LANES
    whole = pl.BlockSpec(memory_space=pltpu.VMEM)
    away = pl.BlockSpec(memory_space=pltpu.HBM)
    return pl.pallas_call(
        functools.partial(message_kernel, local_levels, inner_bits),
        in_specs=[away] * 4,
        out_specs=[whole] * inner_bits,
        out_shape=[jax.ShapeDtypeStruct((rows, LANES), jnp.int16)] * inner_bits,
        scratch_shapes=[
            pltpu.VMEM((leaves, heights, rank, LEAF), jnp.bfloat16),
            pltpu.VMEM((leaves, count, LEAF), jnp.bfloat16),
            pltpu.VMEM((3, points), jnp.float32),
            pltpu.VMEM((1, points), jnp.float32),
            pltpu.SemaphoreType.DMA((leaves,)),
            pltpu.SemaphoreType.DMA((leaves,)),
            pltpu.SemaphoreType.DMA((2,)),
        ],
        compiler_params=pltpu.CompilerParams(vmem_limit_bytes=56 * MIB),
        cost_estimate=pl.CostEstimate(
            flops=2 * heights * rank * count * points,
            bytes_accessed=2 * points * (heights * rank + count + 8),
            transcendentals=0,
        ),
    )(factors, probes, coords, noise.reshape(1, points))


def sums_kernel(rank, points, chips, *refs):
    near_refs, far_refs = refs[:chips], refs[chips : 2 * chips]
    lower_ref, outer_refs = refs[2 * chips], refs[2 * chips + 1 :]
    count = lower_ref.shape[0]
    inner_bits = lower_ref.shape[1] // rank
    parts = 1 + len(outer_refs)
    wide = message_width(rank, len(outer_refs))
    lower = [None] * inner_bits
    outer = [None] * len(outer_refs)

    def added(total, value):
        return value if total is None else total + value

    for chip in range(chips):
        for ref in (near_refs[chip], far_refs[chip]):
            body = ref[4 * points // LANES :].astype(jnp.int32).astype(jnp.float32)
            body = jnp.concatenate(
                [body[:, at : at + wide] for at in range(0, LANES, wide)], axis=0
            )
            powers = jnp.exp2(body[:parts, parts * rank : (parts + 1) * rank]) * (1.0 / COEFF_STEPS)
            scales = jnp.concatenate([powers[part : part + 1] for part in range(parts)], axis=1)
            values = body[:, : parts * rank] * scales
            if chip > 0 or ref is far_refs[chip]:
                height = chip.bit_length()
                lower[height] = added(lower[height], values[:, :rank])
            for at in range(len(outer)):
                outer[at] = added(outer[at], values[:, (1 + at) * rank : (2 + at) * rank])
    lower_ref[...] = jnp.concatenate(lower, axis=1).astype(jnp.bfloat16)
    for ref, value in zip(outer_refs, outer):
        ref[...] = value


def group_sums(near, far, rank, points, count, inner_bits, outer_bits):
    whole = pl.BlockSpec(memory_space=pltpu.VMEM)
    lower, *outer = pl.pallas_call(
        functools.partial(sums_kernel, rank, points, len(near)),
        in_specs=[whole] * (2 * len(near)),
        out_specs=[whole] * (1 + outer_bits),
        out_shape=[jax.ShapeDtypeStruct((count, inner_bits * rank), jnp.bfloat16)]
        + [jax.ShapeDtypeStruct((count, rank), jnp.float32)] * outer_bits,
        compiler_params=pltpu.CompilerParams(vmem_limit_bytes=4 * MIB),
    )(*near, *far)
    return lower, outer


def norm_pieces(value):
    high = value.astype(jnp.bfloat16).astype(jnp.float32)
    rest = value - high
    middle = rest.astype(jnp.bfloat16).astype(jnp.float32)
    return [high, middle, rest - middle]


def gather_kernel(chips, me_ref, order_ref, *refs):
    near_refs, far_refs = refs[:chips], refs[chips : 2 * chips]
    across_ref, along_ref, extra_ref, table = refs[2 * chips :]
    points = order_ref.shape[1]
    rows = 4 * points // LANES
    sub = rows // 4
    shards = 2 * chips
    for shard in range(shards):
        source = (near_refs if shard % 2 == 0 else far_refs)[shard // 2]
        whole = source[:rows].astype(jnp.int32) + int(OFFSET)
        high = (whole >> 8).astype(jnp.float32).astype(jnp.bfloat16)
        low = (whole & 255).astype(jnp.float32).astype(jnp.bfloat16)
        table[2 * rows * shard : 2 * rows * shard + rows, :] = high
        table[2 * rows * shard + rows : 2 * rows * (shard + 1), :] = low

    picks = order_ref[...] ^ (me_ref[0] * points)
    lanes = picks & (LANES - 1)
    lines = picks // LANES

    def lookup(start):
        hot = jnp.where(
            lax.broadcasted_iota(jnp.int32, (LANES, TILE), 0) == lanes[:, start : start + TILE],
            1.0,
            0.0,
        ).astype(jnp.bfloat16)
        return jnp.dot(table[...], hot, preferred_element_type=jnp.float32)

    def select(start, looked):
        span = slice(start, start + TILE)
        place = lines[:, span] - lax.broadcasted_iota(jnp.int32, (sub, TILE), 0)
        totals = [jnp.zeros((sub, TILE), jnp.float32) for _ in range(8)]
        for shard in range(shards):
            here = place == shard * sub
            for which in range(8):
                at = 2 * rows * shard + which * sub
                totals[which] = jnp.where(here, looked[at : at + sub], totals[which])
        found = [jnp.sum(total, axis=0, keepdims=True) for total in totals]
        blank = jnp.zeros((5, TILE), jnp.float32)
        high = (jnp.concatenate(found[:3] + [blank], axis=0) - COORD_MIDDLE) * (256.0 * FEATURE_STEP)
        low = jnp.concatenate(found[4:7] + [blank], axis=0) * FEATURE_STEP
        real = lax.broadcasted_iota(jnp.int32, (8, TILE), 0) < 3
        high = jnp.where(real, high, 0.0)
        value = high + low
        norm = norm_pieces(jnp.sum(value * value, axis=0, keepdims=True))
        ones = jnp.ones((3, TILE), jnp.float32)
        pad = jnp.zeros((2, TILE), jnp.float32)
        none = jnp.zeros((8, TILE), jnp.float32)
        across_ref[:, span] = jnp.concatenate(
            [-2.0 * high, -2.0 * low, -2.0 * high, -2.0 * low] + [ones] + norm + [pad, none], axis=0
        ).astype(jnp.bfloat16)
        along = jnp.concatenate([high, high, low, low] + norm + [ones, pad, none], axis=0)
        along_ref[span, :] = along.T.astype(jnp.bfloat16)
        spread = (found[3] * 256.0 + found[7]) * (1.0 / NOISE_SCALE)
        extra_ref[:, span] = (1.0 + spread).astype(jnp.bfloat16).astype(jnp.float32) - 1.0

    starts = list(range(0, points, TILE))
    looked = lookup(starts[0])
    for start in starts[1:]:
        ahead = lookup(start)
        select(start - TILE, looked)
        looked = ahead
    select(starts[-1], looked)


def gathered(me, order, near, far):
    points = order.shape[1]
    chips = len(near)
    whole = pl.BlockSpec(memory_space=pltpu.VMEM)
    return pl.pallas_call(
        functools.partial(gather_kernel, chips),
        in_specs=[pl.BlockSpec(memory_space=pltpu.SMEM)] + [whole] * (1 + 2 * chips),
        out_specs=[whole] * 3,
        out_shape=[
            jax.ShapeDtypeStruct((48, points), jnp.bfloat16),
            jax.ShapeDtypeStruct((points, 48), jnp.bfloat16),
            jax.ShapeDtypeStruct((1, points), jnp.float32),
        ],
        scratch_shapes=[pltpu.VMEM((16 * chips * points // LANES, LANES), jnp.bfloat16)],
        compiler_params=pltpu.CompilerParams(vmem_limit_bytes=16 * MIB),
        cost_estimate=pl.CostEstimate(
            flops=32 * points * chips * points, bytes_accessed=points * 36, transcendentals=0
        ),
    )(me, order, *near, *far)


def dense_kernel(
    across_ref, along_ref, extra_ref, probes_ref, factors_ref, lower_ref, *rest
):
    outer_refs = rest[:-9]
    out_ref, vectors, left, right, blocks, squares, totals, in_sems, out_sems = rest[-9:]
    levels, _, rank, points = factors_ref.shape
    leaves = points // LEAF
    local_levels = right.shape[0]
    arriving = [
        pltpu.make_async_copy(probes_ref, vectors, in_sems.at[0]),
        pltpu.make_async_copy(
            factors_ref.at[pl.ds(0, local_levels), 1], right, in_sems.at[1 + leaves]
        ),
    ]
    for leaf in range(leaves):
        arriving.append(
            pltpu.make_async_copy(
                factors_ref.at[:, 0, :, pl.ds(leaf * LEAF, LEAF)],
                left.at[leaf],
                in_sems.at[1 + leaf],
            )
        )
    for copy in arriving:
        copy.start()

    upper = [lower_ref[...].astype(jnp.float32)]
    for bit in range(len(outer_refs).bit_length()):
        arrived = [ref[...] for ref in outer_refs[(1 << bit) - 1 : (2 << bit) - 1]]
        upper.append(functools.reduce(jnp.add, arrived))
    upper = jnp.concatenate(upper, axis=1)

    def distances(slot, leaf, column):
        base, last = leaf * LEAF, column + TILE
        squares[slot, :last] = jnp.dot(
            along_ref[base : base + last],
            across_ref[:, base + column : base + last],
            preferred_element_type=jnp.float32,
        )

    def entries(slot, leaf, column):
        for row in range(0, column + TILE, STRIP):
            skip = max(row - column, 0)
            square = jnp.maximum(squares[slot, row : row + STRIP, skip:], 1e-30)
            scaled = square * lax.rsqrt(square)
            value = (scaled + 1.0 / LN_2) * jnp.exp2(LOG2_LN_2 - scaled)
            blocks[leaf, row : row + STRIP, column + skip : column + TILE] = value.astype(
                jnp.bfloat16
            )
            if row == column:
                mirrored = value[:, STRIP:].T.astype(jnp.bfloat16)
                blocks[leaf, row + STRIP : row + TILE, column : column + STRIP] = mirrored

    def products(leaf, column):
        base, last = leaf * LEAF, column + TILE
        here = vectors[:, base + column : base + last]
        total = here.astype(jnp.float32) * extra_ref[:, base + column : base + last]
        totals[leaf, :, column:last] = total + jnp.dot(
            vectors[:, base : base + last],
            blocks[leaf, :last, column:last],
            preferred_element_type=jnp.float32,
        )
        if column > 0:
            totals[leaf, :, :column] += lax.dot_general(
                here,
                blocks[leaf, :column, column:last],
                (((1,), (1,)), ((), ())),
                preferred_element_type=jnp.float32,
            )

    def own_coefficients(leaf):
        span = slice(leaf * LEAF, (leaf + 1) * LEAF)
        return lax.dot_general(
            right[:, :, span].reshape(local_levels * rank, LEAF),
            vectors[:, span],
            (((1,), (1,)), ((), ())),
            preferred_element_type=jnp.float32,
        )

    def local_siblings(leaf, coeffs):
        parts = []
        for level in range(local_levels):
            node = (leaf >> level) ^ 1
            members = coeffs[node << level : (node + 1) << level]
            parts.append(functools.reduce(jnp.add, members)[level * rank : (level + 1) * rank])
        return jnp.concatenate(parts, axis=0).T

    def low_rank(leaf):
        both = jnp.concatenate([local_siblings(leaf, coeffs), upper], axis=1)
        totals[leaf] += jnp.dot(
            both.astype(jnp.bfloat16),
            left[leaf].reshape(levels * rank, LEAF),
            preferred_element_type=jnp.float32,
        )

    leaving = []
    coeffs = []
    ready = None
    order = [(leaf, column) for leaf in range(leaves) for column in range(0, LEAF, TILE)]
    distances(0, *order[0])
    for at, (leaf, column) in enumerate(order):
        if at + 1 < len(order):
            distances((at + 1) % 2, *order[at + 1])
        entries(at % 2, leaf, column)
        if ready is not None:
            if ready == (0, 0):
                for copy in arriving:
                    copy.wait()
                coeffs = [own_coefficients(each) for each in range(leaves)]
            products(*ready)
            if ready[1] + TILE == LEAF:
                low_rank(ready[0])
                leaving.append(sent_out(totals, out_ref, out_sems, ready[0]))
        ready = (leaf, column)
    products(*ready)
    low_rank(ready[0])
    leaving.append(sent_out(totals, out_ref, out_sems, ready[0]))
    for copy in leaving:
        copy.wait()


def sent_out(totals, out_ref, sems, leaf):
    copy = pltpu.make_async_copy(
        totals.at[leaf], out_ref.at[:, pl.ds(leaf * LEAF, LEAF)], sems.at[leaf]
    )
    copy.start()
    return copy


def assembled(features, probes, factors, lower, outer, local_levels):
    count, points = probes.shape
    levels, _, rank, _ = factors.shape
    leaves = points // LEAF
    whole = pl.BlockSpec(memory_space=pltpu.VMEM)
    away = pl.BlockSpec(memory_space=pltpu.HBM)
    return pl.pallas_call(
        dense_kernel,
        in_specs=[whole, whole, whole, away, away, whole] + [whole] * len(outer),
        out_specs=away,
        out_shape=jax.ShapeDtypeStruct((count, points), jnp.float32),
        scratch_shapes=[
            pltpu.VMEM((count, points), jnp.bfloat16),
            pltpu.VMEM((leaves, levels, rank, LEAF), jnp.bfloat16),
            pltpu.VMEM((local_levels, rank, points), jnp.bfloat16),
            pltpu.VMEM((leaves, LEAF, LEAF), jnp.bfloat16),
            pltpu.VMEM((2, LEAF, TILE), jnp.float32),
            pltpu.VMEM((leaves, count, LEAF), jnp.float32),
            pltpu.SemaphoreType.DMA((2 + leaves,)),
            pltpu.SemaphoreType.DMA((leaves,)),
        ],
        compiler_params=pltpu.CompilerParams(vmem_limit_bytes=32 * MIB),
        cost_estimate=pl.CostEstimate(
            flops=2 * points * (LEAF * count + levels * rank * count),
            bytes_accessed=points * (2 * levels * rank + 6 * count),
            transcendentals=points * LEAF,
        ),
    )(*features, probes, factors, lower, *outer)


def local(coords, noise, order, probes, factors):
    count, points = probes.shape
    rank = factors.shape[2]
    local_levels = (points // LEAF).bit_length() - 1
    inner_bits = lax.axis_size("gy").bit_length() - 1
    outer_bits = lax.axis_size("gx").bit_length() - 1
    sent = messages(coords, noise, factors, probes, local_levels, inner_bits)
    me = lax.axis_index("gy")
    chips = 1 << (inner_bits - 1)
    arrived = {
        chip: exchanged(sent[chip.bit_length()], "gy", 2 * chip) for chip in range(chips - 1, 0, -1)
    }
    own = sent[0] ^ (me >> 8).astype(jnp.int16)
    others = [arrived[chip] for chip in range(1, chips)]
    near = [own] + others
    far = [exchanged(part, "gy", 1) for part in [sent[0]] + others]
    lower, partial = group_sums(near, far, rank, points, count, inner_bits, outer_bits)
    outer = [
        exchanged(partial[mask.bit_length() - 1], "gx", mask) for mask in range(1, 1 << outer_bits)
    ]
    features = gathered(me.reshape(1), order, near, far)
    return assembled(features, probes, factors, lower, outer, local_levels)


def solution(mesh):
    return jax.shard_map(
        local,
        mesh=mesh,
        in_specs=(
            P(None, ("gx", "gy")),
            P(("gx", "gy")),
            P("gx", "gy"),
            P(None, ("gx", "gy")),
            P(None, None, None, ("gx", "gy")),
        ),
        out_specs=P(None, ("gx", "gy")),
        check_vma=False,
    )
```
